32 devices in a mesh: lat: 4 (over z), lon: 8 (over y, x, core).
Axes of the slice: x: 2, y: 2, z: 4, core: 2. Of those that a mesh axis runs over, the one named last changes fastest.
Arguments:
- right_side: float32 [111, 64, 1024], P(None, 'lat', 'lon'), may hold values from -6 to 6
- blocks: float32 [64, 111, 111], P('lat'), as said below
- kappa: float32 [64], P('lat'), may hold values from 0.5 to 4
- fine_ids: int32 [64, 1024], P('lat', 'lon'), may hold values from 0 to 63, as said below
- coarse_ids: int32 [32, 512], P('lat', 'lon'), may hold values from 0 to 31, as said below
Outputs:
- solution: float32 [111, 64, 1024], P(None, 'lat', 'lon')
- residual: float32 [111, 64, 1024], P(None, 'lat', 'lon')
The draws below stay inside these ranges and needn't reach their ends.
Inputs may be any that keep to these rules, and one draw needn't show every extreme that they name: fine_ids[j, c] is (c mod 128) // 2, or one less than that where c is even and (c mod 128) // 2 > 0. coarse_ids[j, c] is (c mod (64)) // 2, or one less than that where c is even and (c mod (64)) // 2 > 0. Each blocks[j] is symmetric, with a diagonal larger than the sum of magnitudes of the rest of its row.
All inputs are finite; a program needn't handle non-finite values.
Results may differ from the reference program's by a relative error of at most 0.0003.
Values sent between devices are 32-bit elements; how exact they have to be, the bound alone decides.
A program may use at most 128 MiB of HBM per device.

```python
import math
import jax
import jax.numpy as jnp
from jax import lax

COMP = 111
CLON = 128
SWEEPS = 2
COARSE_SWEEPS = 4
CYCLES = 2
NLAT = 64
NLON = 1024


def aggregate_columns(key, rows, cols, local_cols):
    column = jnp.arange(cols, dtype=jnp.int32) % local_cols
    box = column // 2
    west = jax.random.randint(key, (rows, cols), 0, 2, dtype=jnp.int32)
    movable = (column % 2 == 0).astype(jnp.int32) * (box > 0).astype(jnp.int32)
    return box[None, :] - west * movable[None, :]


def draw_fine_ids(key, part):
    key = jax.random.fold_in(key, 11)
    return aggregate_columns(key, NLAT, NLON, CLON)


def draw_coarse_ids(key, part):
    key = jax.random.fold_in(key, 23)
    return aggregate_columns(key, NLAT // 2, NLON // 2, CLON // 2)


def draw_blocks(key, part):
    key = jax.random.fold_in(key, 5)
    first, second = jax.random.split(key)
    raw = jax.random.uniform(first, (NLAT, COMP, COMP), jnp.float32, -0.02, 0.02)
    sym = 0.5 * (raw + jnp.swapaxes(raw, 1, 2))
    lift = jax.random.uniform(second, (NLAT, 1, 1), jnp.float32, 0.0, 1.0)
    extra = 1.5 * lift
    eye = jnp.eye(COMP, dtype=jnp.float32)
    return sym * (1.0 - eye) + eye * (0.02 * COMP + 0.1 + extra)


def levels(own_key, shape, cuts, least, top_value):
    gain = 1.0
    for axis_at, shards_of in cuts:
        steps = jax.random.uniform(jax.random.fold_in(jax.random.fold_in(own_key, 6), axis_at), (shards_of,), jnp.float32, least / len(cuts), top_value / len(cuts))
        gain = gain * jnp.repeat(jnp.exp(steps), shape[axis_at] // shards_of).reshape((-1,) + (1,) * (len(shape) - 1 - axis_at))
    return gain


def centred(own_key, dims, scale, most, cuts=(), kind=jnp.bfloat16):
    gain = levels(own_key, dims, cuts, -0.22, 0.18) if cuts else 1.0
    values = jax.random.normal(own_key, dims, jnp.float32) * scale * gain
    return jnp.minimum(jnp.maximum(values, -most), most).astype(kind)


def setup_inputs(seed: int = 0) -> dict:
    streams_of = jax.random.split(jax.random.key(seed), 6)
    return {
        "right_side": centred(streams_of[0], (COMP, NLAT, NLON), 1.0, 6.0, ((1, 4), (2, 8)), jnp.float32),
        "blocks": draw_blocks(jax.random.fold_in(streams_of[5], 71), 0),
        "kappa": jnp.clip(jnp.exp(math.log(4.0) - 2.0794415 * jax.random.uniform(streams_of[2], (NLAT,), jnp.float32) ** levels(streams_of[2], (NLAT,), ((0, 4),), -0.2, 0.2)), 0.5, 4.0),
        "fine_ids": draw_fine_ids(jax.random.fold_in(streams_of[5], 71), 0),
        "coarse_ids": draw_coarse_ids(jax.random.fold_in(streams_of[5], 71), 0),
    }


OMEGA = 0.8
SMOOTH_WEIGHT = 2.0 / 3.0
HIGH = lax.Precision.HIGHEST

def invert_blocks(blocks, kappa):
    width = blocks.shape[1]
    eye = jnp.eye(width, dtype=blocks.dtype)
    shifted = blocks + 4.0 * kappa[:, None, None] * eye
    factor = jnp.linalg.cholesky(shifted)

    def single(lower):
        return jax.scipy.linalg.solve_triangular(lower, eye, lower=True)
    lower_inv = jax.vmap(single)(factor)
    return jnp.einsum('jmk,jml->jkl', lower_inv, lower_inv, precision=HIGH)

def coarsen_tables(blocks, kappa):
    rows = blocks.shape[0] // 2
    grouped = blocks.reshape(rows, 2, blocks.shape[1], blocks.shape[2])
    return (4.0 * jnp.mean(grouped, axis=1), 2.0 * jnp.mean(kappa.reshape(rows, 2), axis=1))

def block_apply(blocks, field):
    return jnp.einsum('jkm,mjl->kjl', blocks, field, precision=HIGH)

def operate(field, blocks, kappa):
    padded = jnp.pad(field, ((0, 0), (1, 1), (0, 0)))
    beside_all = padded[:, :-2, :] + padded[:, 2:, :] + jnp.roll(field, 1, axis=2) + jnp.roll(field, -1, axis=2)
    return block_apply(blocks, field) + kappa[None, :, None] * (4.0 * field - beside_all)

def relax(guess, rhs, blocks, kappa, inverse, count):
    for sweep in range(count):
        if guess is None:
            guess = OMEGA * block_apply(inverse, rhs)
        else:
            guess = guess + OMEGA * block_apply(inverse, rhs - operate(guess, blocks, kappa))
    return guess

def global_columns(ids, local_cols):
    sector = jnp.arange(ids.shape[1], dtype=jnp.int32) // local_cols
    return ids + sector[None, :] * (local_cols // 2)

def flat_index(gcol, coarse_cols):
    rows = gcol.shape[0]
    return jnp.arange(rows, dtype=jnp.int32)[:, None] // 2 * coarse_cols + gcol

def restrict(field, gcol):
    width, rows, cols = field.shape
    coarse_cols = cols // 2
    index = flat_index(gcol, coarse_cols)
    flat = field.reshape(width, rows * cols).T
    summed = jax.ops.segment_sum(flat, index.reshape(-1), num_segments=rows // 2 * coarse_cols)
    return summed.T.reshape(width, rows // 2, coarse_cols)

def prolong(coarse, gcol):
    width, crow, ccol = coarse.shape
    index = flat_index(gcol, ccol)
    flat = coarse.reshape(width, crow * ccol)
    return jnp.take(flat, index, axis=1)

def reference(right_side, blocks, kappa, fine_ids, coarse_ids):
    inv0 = invert_blocks(blocks, kappa)
    blocks1, kappa1 = coarsen_tables(blocks, kappa)
    inv1 = invert_blocks(blocks1, kappa1)
    blocks2, kappa2 = coarsen_tables(blocks1, kappa1)
    inv2 = invert_blocks(blocks2, kappa2)
    gcol0 = global_columns(fine_ids, CLON)
    gcol1 = global_columns(coarse_ids, CLON // 2)

    def level_one(rhs):
        smooth = relax(None, rhs, blocks1, kappa1, inv1, SWEEPS)
        resid = rhs - operate(smooth, blocks1, kappa1)
        coarse = relax(None, restrict(resid, gcol1), blocks2, kappa2, inv2, COARSE_SWEEPS)
        smooth = smooth + prolong(coarse, gcol1)
        return relax(smooth, rhs, blocks1, kappa1, inv1, SWEEPS)

    def level_zero(rhs):
        smooth = relax(None, rhs, blocks, kappa, inv0, SWEEPS)
        resid = rhs - operate(smooth, blocks, kappa)
        damped = resid - SMOOTH_WEIGHT * operate(block_apply(inv0, resid), blocks, kappa)
        correction = prolong(level_one(restrict(damped, gcol0)), gcol0)
        correction = correction - SMOOTH_WEIGHT * block_apply(inv0, operate(correction, blocks, kappa))
        smooth = smooth + correction
        return relax(smooth, rhs, blocks, kappa, inv0, SWEEPS)
    solution = level_zero(right_side)
    for cycle in range(CYCLES - 1):
        solution = solution + level_zero(right_side - operate(solution, blocks, kappa))
    residual = right_side - operate(solution, blocks, kappa)
    return (solution, residual)
```

```python
import jax
import jax.numpy as jnp
from jax import lax
from jax.experimental import pallas as pl
from jax.experimental.pallas import tpu as pltpu
from jax.sharding import PartitionSpec as P

SWEEPS = 2
COARSE_SWEEPS = 4


OMEGA = 0.8
SMOOTH_WEIGHT = 2.0 / 3.0
HIGH = lax.Precision.HIGHEST


def padded_2(block, sides, width, periodic):
    for axis, dim in sides:
        count = lax.axis_size(axis)
        forward = [(i, i + 1) for i in range(count - 1)]
        if periodic:
            forward.append((count - 1, 0))
        backward = [(target, source) for source, target in forward]
        low = lax.ppermute(
            lax.slice_in_dim(block, block.shape[dim] - width, None, axis=dim), axis, forward
        )
        high = lax.ppermute(lax.slice_in_dim(block, 0, width, axis=dim), axis, backward)
        block = jnp.concatenate([low, block, high], axis=dim)
    return block


def invert_kernel(width, m_ref, out_ref, work):
    count, rows, lanes = work.shape
    work[...] = m_ref[...]
    lane_row = lax.broadcasted_iota(jnp.int32, (1, lanes), 1)
    lane_all = lax.broadcasted_iota(jnp.int32, (rows, lanes), 1)

    def step(k, carry):
        at_row = lane_row == k
        at_all = lane_all == k
        index = jnp.full((rows, lanes), k, jnp.int32)
        index_row = jnp.full((1, lanes), k, jnp.int32)
        for m in range(count):
            mat = work[m]
            row = work[m, pl.ds(k, 1), :]
            pivot = jnp.sum(jnp.where(at_row, row, 0.0), axis=1, keepdims=True)
            inv = 1.0 / pivot
            row = jnp.where(at_row, inv, row * inv)
            col = jnp.take_along_axis(mat, index, axis=1)
            work[m] = jnp.where(at_all, 0.0, mat) - col * row
            work[m, pl.ds(k, 1), :] = row
        return carry

    lax.fori_loop(0, width, step, 0)
    out_ref[...] = work[...]


def invert_stack(mats, width):
    return pl.pallas_call(
        lambda *refs: invert_kernel(width, *refs),
        out_shape=jax.ShapeDtypeStruct(mats.shape, jnp.float32),
        in_specs=[pl.BlockSpec(memory_space=pltpu.VMEM)],
        out_specs=pl.BlockSpec(memory_space=pltpu.VMEM),
        scratch_shapes=[pltpu.VMEM(mats.shape, jnp.float32)],
        compiler_params=pltpu.CompilerParams(vmem_limit_bytes=32 * 1024 * 1024),
        name="invert",
    )(mats)


def invert_levels(tables):
    width = tables[0][0].shape[1]
    eye = jnp.eye(width, dtype=jnp.float32)
    shifted = jnp.concatenate(
        [pair[0] + 4.0 * pair[1][:, None, None] * eye for pair in tables], axis=0
    )
    tall = -(-width // 8) * 8
    wide = -(-width // 128) * 128
    padded = jnp.pad(shifted, ((0, 0), (0, tall - width), (0, wide - width)))
    inverse = invert_stack(padded, width)[:, :width, :width]
    pieces = []
    offset = 0
    for pair in tables:
        count = pair[0].shape[0]
        pieces.append(inverse[offset : offset + count])
        offset = offset + count
    return pieces


def coarsen_tables(blocks, kappa):
    rows = blocks.shape[0] // 2
    grouped = blocks.reshape(rows, 2, blocks.shape[1], blocks.shape[2])
    return (4.0 * jnp.mean(grouped, axis=1), 2.0 * jnp.mean(kappa.reshape(rows, 2), axis=1))


def block_apply(blocks, field):
    return jnp.einsum("jkm,mjl->kjl", blocks, field, precision=HIGH)


def neighbour_sum(field):
    padded = padded_2(field, (("lat", 1),), 1, False)
    circle = padded_2(field, (("lon", 2),), 1, True)
    return padded[:, :-2, :] + padded[:, 2:, :] + circle[:, :, :-2] + circle[:, :, 2:]


def operate(field, blocks, kappa):
    beside_all = neighbour_sum(field)
    return block_apply(blocks, field) + kappa[None, :, None] * (4.0 * field - beside_all)


def relax(guess, rhs, blocks, kappa, inverse, count):
    for sweep in range(count):
        if guess is None:
            guess = OMEGA * block_apply(inverse, rhs)
        else:
            update = rhs - operate(guess, blocks, kappa)
            guess = guess + OMEGA * block_apply(inverse, update)
    return guess


def aggregation_table(ids):
    rows, cols = ids.shape
    grouped = ids.reshape(rows // 2, 2, cols)
    targets = jnp.arange(cols // 2, dtype=jnp.int32)
    return (grouped[..., None] == targets).astype(jnp.float32)


def restrict(field, table):
    width, rows, cols = field.shape
    grouped = field.reshape(width, rows // 2, 2, cols)
    return jnp.einsum("kprl,prlc->kpc", grouped, table, precision=HIGH)


def prolong(coarse, table):
    fine = jnp.einsum("kpc,prlc->kprl", coarse, table, precision=HIGH)
    width, pairs, two, cols = fine.shape
    return fine.reshape(width, pairs * two, cols)


def per_device(right_side, blocks, kappa, fine_ids, coarse_ids):
    blocks1, kappa1 = coarsen_tables(blocks, kappa)
    blocks2, kappa2 = coarsen_tables(blocks1, kappa1)
    table0 = aggregation_table(fine_ids)
    table1 = aggregation_table(coarse_ids)
    inv0, inv1, inv2 = invert_levels([(blocks, kappa), (blocks1, kappa1), (blocks2, kappa2)])

    def coarsest(rhs):
        return relax(None, rhs, blocks2, kappa2, inv2, COARSE_SWEEPS)

    def level_one(rhs):
        smooth = relax(None, rhs, blocks1, kappa1, inv1, SWEEPS)
        resid = rhs - operate(smooth, blocks1, kappa1)
        smooth = smooth + prolong(coarsest(restrict(resid, table1)), table1)
        return relax(smooth, rhs, blocks1, kappa1, inv1, SWEEPS)

    def level_zero(rhs):
        smooth = relax(None, rhs, blocks, kappa, inv0, SWEEPS)
        resid = rhs - operate(smooth, blocks, kappa)
        damped = resid - SMOOTH_WEIGHT * operate(block_apply(inv0, resid), blocks, kappa)
        correction = prolong(level_one(restrict(damped, table0)), table0)
        correction = correction - SMOOTH_WEIGHT * block_apply(
            inv0, operate(correction, blocks, kappa)
        )
        smooth = smooth + correction
        return relax(smooth, rhs, blocks, kappa, inv0, SWEEPS)

    solution = level_zero(right_side)
    solution = solution + level_zero(right_side - operate(solution, blocks, kappa))
    residual = right_side - operate(solution, blocks, kappa)
    return (solution, residual)


def solution(mesh):
    in_specs = (
        P(None, "lat", "lon"),
        P("lat", None, None),
        P("lat"),
        P("lat", "lon"),
        P("lat", "lon"),
    )
    out_specs = (P(None, "lat", "lon"), P(None, "lat", "lon"))
    return jax.shard_map(
        per_device, mesh=mesh, in_specs=in_specs, out_specs=out_specs, check_vma=False
    )
```

```python
import functools

import jax
import jax.numpy as jnp
from jax import lax
from jax.experimental import pallas as pl
from jax.experimental.pallas import tpu as pltpu
from jax.sharding import PartitionSpec as P

SWEEPS = 2
COARSE_SWEEPS = 4
CYCLES = 2
OMEGA = 0.8
SMOOTH_WEIGHT = 2.0 / 3.0
HIGH = lax.Precision.HIGHEST
EDGE = 8
GROUP = 4


def invert_kernel(width, m_ref, out_ref):
    rows, count, lanes = m_ref.shape
    out_ref[...] = m_ref[...]
    lane = lax.broadcasted_iota(jnp.int32, (count, lanes), 1)

    def step(k, carry):
        at = lane == k
        index = jnp.full((count, lanes), k, jnp.int32)
        row = out_ref[k]
        inv = 1.0 / jnp.take_along_axis(row, index, axis=1)
        row = jnp.where(at, inv, row * inv)
        for i in range(rows):
            mat = out_ref[i]
            col = jnp.take_along_axis(mat, index, axis=1)
            out_ref[i] = jnp.where(at, 0.0, mat) - col * row
        out_ref[k] = row
        return carry

    lax.fori_loop(0, width, step, 0)


def invert_stack(mats, width):
    return pl.pallas_call(
        functools.partial(invert_kernel, width),
        out_shape=jax.ShapeDtypeStruct(mats.shape, jnp.float32),
        in_specs=[pl.BlockSpec(memory_space=pltpu.VMEM)],
        out_specs=pl.BlockSpec(memory_space=pltpu.VMEM),
        compiler_params=pltpu.CompilerParams(vmem_limit_bytes=32 * 1024 * 1024),
        name="invert",
    )(mats)


def cycle_kernel(
    nlat, nlon, rhs, w0, w1, w2, m0, k0, k1, k2, down0, up0, down1, up1,
    sol, res, va, vb, va1, vb1, va2, vb2, x0, r0, b1, x1, r1, x2, r2,
    lat_recv, lon_send, lon_recv, send_sem, recv_sem,
):
    lat = lax.axis_index("lat")
    lon = lax.axis_index("lon")
    west = lax.rem(lon + nlon - 1, nlon)
    east = lax.rem(lon + 1, nlon)
    has_north = lat > 0
    has_south = lat < nlat - 1
    rows, cols, lanes = rhs.shape

    lat_recv[...] = jnp.zeros_like(lat_recv)
    lon_send[...] = jnp.zeros_like(lon_send)

    barrier = pltpu.get_barrier_semaphore()
    for side in (west, east):
        pl.semaphore_signal(
            barrier, inc=1, device_id=(lat, side), device_id_type=pl.DeviceIdType.MESH
        )

    @pl.when(has_north)
    def _():
        pl.semaphore_signal(
            barrier, inc=1, device_id=(lat - 1, lon), device_id_type=pl.DeviceIdType.MESH
        )

    @pl.when(has_south)
    def _():
        pl.semaphore_signal(
            barrier, inc=1, device_id=(lat + 1, lon), device_id_type=pl.DeviceIdType.MESH
        )

    peers = 2 + jnp.minimum(lat, 1) + jnp.minimum(nlat - 1 - lat, 1)
    pl.semaphore_wait(barrier, peers)

    def each(count, body):
        group = min(GROUP, count)

        def some(g, carry):
            for i in range(group):
                body(g * group + i)
            return carry

        lax.fori_loop(0, count // group, some, 0)

    def copies(field, par):
        high = field.shape[0] - 2
        wide = field.shape[1] - 2 * EDGE
        tall = max(high, 8)

        def make(src, dst, which, target):
            return pltpu.make_async_remote_copy(
                src_ref=src, dst_ref=dst,
                send_sem=send_sem.at[par, which], recv_sem=recv_sem.at[par, which],
                device_id=target, device_id_type=pl.DeviceIdType.MESH,
            )

        inner = pl.ds(EDGE, wide)
        return (
            make(field.at[1, inner], lat_recv.at[par, 1, pl.ds(0, wide)], 0, (lat - 1, lon)),
            make(field.at[high, inner], lat_recv.at[par, 0, pl.ds(0, wide)], 1, (lat + 1, lon)),
            make(lon_send.at[par, 0, pl.ds(0, tall)], lon_recv.at[par, 1, pl.ds(0, tall)], 2, (lat, west)),
            make(lon_send.at[par, 1, pl.ds(0, tall)], lon_recv.at[par, 0, pl.ds(0, tall)], 3, (lat, east)),
        )

    def start(field, par):
        north, south, left, right = copies(field, par)
        left.start()
        right.start()
        pl.when(has_north)(north.start)
        pl.when(has_south)(south.start)

    def finish(field, par):
        north, south, left, right = copies(field, par)
        high = field.shape[0] - 2
        wide = field.shape[1] - 2 * EDGE
        left.wait()
        right.wait()

        @pl.when(has_north)
        def _():
            north.wait_send()
            south.wait_recv()

        @pl.when(has_south)
        def _():
            south.wait_send()
            north.wait_recv()

        inner = pl.ds(EDGE, wide)
        field[0, inner] = lat_recv[par, 0, pl.ds(0, wide)]
        field[high + 1, inner] = lat_recv[par, 1, pl.ds(0, wide)]
        for j in range(high):
            field[j + 1, pl.ds(EDGE - 1, 1)] = lon_recv[par, 0, pl.ds(j, 1)]
            field[j + 1, pl.ds(EDGE + wide, 1)] = lon_recv[par, 1, pl.ds(j, 1)]

    def put(field, par, j, value):
        wide = value.shape[0]
        field[j + 1, pl.ds(EDGE, wide)] = value
        lon_send[par, 0, pl.ds(j, 1)] = value[:1]
        lon_send[par, 1, pl.ds(j, 1)] = value[wide - 1 :]

    def beside(field, kap, j):
        wide = field.shape[1] - 2 * EDGE
        inner = pl.ds(EDGE, wide)
        total = field[j, inner] + field[j + 2, inner]
        total += field[j + 1, pl.ds(EDGE - 1, wide)] + field[j + 1, pl.ds(EDGE + 1, wide)]
        return kap[j] * total

    def split(value):
        top = value.astype(jnp.bfloat16)
        return top, (value - top.astype(jnp.float32)).astype(jnp.bfloat16)

    def solve(weights, j, value):
        top, low = split(value)
        return jnp.dot(
            jnp.concatenate([top, low, top], axis=1), weights[j],
            preferred_element_type=jnp.float32,
        )

    def select(table, value):
        top, low = split(value)
        return jnp.dot(table, top, preferred_element_type=jnp.float32) + jnp.dot(
            table, low, preferred_element_type=jnp.float32
        )

    def swap(field, par):
        start(field, par)
        finish(field, par)

    res[...] = rhs[...]
    sol[...] = jnp.zeros_like(sol)

    def cycle(_, carry):
        def first(j):
            d = OMEGA * solve(w0, j, res[j])
            x0[j] = d
            put(va, 0, j, d)

        each(rows, first)
        swap(va, 0)

        def second(j):
            r = (1.0 - OMEGA) * res[j] + beside(va, k0, j)
            r0[j] = r
            d = OMEGA * solve(w0, j, r)
            x0[j] = x0[j] + d
            put(vb, 1, j, d)

        each(rows, second)
        swap(vb, 1)

        def third(j):
            r = (1.0 - OMEGA) * r0[j] + beside(vb, k0, j)
            r0[j] = r
            put(va, 0, j, solve(w0, j, r))

        each(rows, third)
        swap(va, 0)

        def fourth(p):
            q = [
                (1.0 - SMOOTH_WEIGHT) * r0[2 * p + i]
                + SMOOTH_WEIGHT * beside(va, k0, 2 * p + i)
                for i in range(2)
            ]
            b = select(down0[p], jnp.concatenate(q, axis=0))
            b1[p] = b
            d = OMEGA * solve(w1, p, b)
            x1[p] = d
            put(va1, 1, p, d)

        each(rows // 2, fourth)
        swap(va1, 1)

        def fifth(j):
            r = (1.0 - OMEGA) * b1[j] + beside(va1, k1, j)
            r1[j] = r
            d = OMEGA * solve(w1, j, r)
            x1[j] = x1[j] + d
            put(vb1, 0, j, d)

        each(rows // 2, fifth)
        swap(vb1, 0)

        def sixth(p):
            q = [
                (1.0 - OMEGA) * r1[2 * p + i] + beside(vb1, k1, 2 * p + i)
                for i in range(2)
            ]
            b = select(down1[p], jnp.concatenate(q, axis=0))
            r2[p] = b
            d = OMEGA * solve(w2, p, b)
            x2[p] = d
            put(va2, 1, p, d)

        each(rows // 4, sixth)
        swap(va2, 1)

        here, there, par = va2, vb2, 0
        for sweep in range(1, COARSE_SWEEPS):
            last = sweep == COARSE_SWEEPS - 1

            def coarse(j, here=here, there=there, par=par, last=last):
                r = (1.0 - OMEGA) * r2[j] + beside(here, k2, j)
                r2[j] = r
                d = OMEGA * solve(w2, j, r)
                x2[j] = x2[j] + d
                if not last:
                    put(there, par, j, d)

            each(rows // 4, coarse)
            if not last:
                swap(there, par)
                here, there, par = there, here, 1 - par

        def seventh(p):
            wide = x1.shape[1]
            up = select(up1[p], x2[p])
            for i in range(2):
                x = x1[2 * p + i] + up[i * wide : (i + 1) * wide]
                x1[2 * p + i] = x
                put(va1, 0, 2 * p + i, x)

        each(rows // 4, seventh)
        swap(va1, 0)

        def eighth(j):
            x = (1.0 - OMEGA) * x1[j] + OMEGA * solve(w1, j, b1[j] + beside(va1, k1, j))
            x1[j] = x
            put(vb1, 1, j, x)

        each(rows // 2, eighth)
        swap(vb1, 1)

        def ninth(p):
            x = (1.0 - OMEGA) * x1[p] + OMEGA * solve(w1, p, b1[p] + beside(vb1, k1, p))
            up = select(up0[p], x)
            for i in range(2):
                put(vb, 0, 2 * p + i, up[i * cols : (i + 1) * cols])

        each(rows // 2, ninth)
        swap(vb, 0)

        def tenth(j):
            e = vb[j + 1, pl.ds(EDGE, cols)]
            x = x0[j] + (1.0 - SMOOTH_WEIGHT) * e
            x += SMOOTH_WEIGHT * solve(w0, j, beside(vb, k0, j))
            x0[j] = x
            put(va, 1, j, x)

        each(rows, tenth)
        swap(va, 1)

        def eleventh(j):
            x = (1.0 - OMEGA) * x0[j] + OMEGA * solve(w0, j, res[j] + beside(va, k0, j))
            x0[j] = x
            put(vb, 0, j, x)

        each(rows, eleventh)
        swap(vb, 0)

        def twelfth(j):
            x = (1.0 - OMEGA) * x0[j] + OMEGA * solve(w0, j, res[j] + beside(vb, k0, j))
            x0[j] = x
            sol[j] = sol[j] + x
            put(va, 1, j, x)

        each(rows, twelfth)
        start(va, 1)

        def product(j):
            res[j] = res[j] - jnp.dot(
                x0[j], m0[j], precision=HIGH, preferred_element_type=jnp.float32
            )

        each(rows, product)
        finish(va, 1)

        def remainder(j):
            res[j] = res[j] + beside(va, k0, j)

        each(rows, remainder)
        return carry

    lax.fori_loop(0, CYCLES, cycle, 0)


def coarsen_tables(blocks, kappa):
    rows = blocks.shape[0] // 2
    grouped = blocks.reshape(rows, 2, blocks.shape[1], blocks.shape[2])
    return (4.0 * jnp.mean(grouped, axis=1), 2.0 * jnp.mean(kappa.reshape(rows, 2), axis=1))


def aggregation_tables(ids):
    rows, cols = ids.shape
    flat = ids.reshape(rows // 2, 2 * cols)
    targets = jnp.arange(cols // 2, dtype=jnp.int32)
    down = (flat[:, None, :] == targets[None, :, None]).astype(jnp.bfloat16)
    up = (flat[:, :, None] == targets).astype(jnp.bfloat16)
    return down, up


def per_device(nlat, nlon, right_side, blocks, kappa, fine_ids, coarse_ids):
    comp, rows, cols = right_side.shape
    lanes = -(-comp // 128) * 128
    tall = -(-comp // 8) * 8
    blocks1, kappa1 = coarsen_tables(blocks, kappa)
    blocks2, kappa2 = coarsen_tables(blocks1, kappa1)
    eye = jnp.eye(comp, dtype=jnp.float32)
    shifted = jnp.concatenate(
        [
            b + 4.0 * k[:, None, None] * eye
            for b, k in ((blocks, kappa), (blocks1, kappa1), (blocks2, kappa2))
        ],
        axis=0,
    )
    total = shifted.shape[0]
    batch = -(-total // 8) * 8
    filler = jnp.broadcast_to(eye, (batch - total, comp, comp))
    stacked = jnp.transpose(jnp.concatenate([shifted, filler], axis=0), (1, 0, 2))
    stacked = jnp.pad(stacked, ((0, tall - comp), (0, 0), (0, lanes - comp)))
    inverse = jnp.transpose(invert_stack(stacked, comp)[:, :total], (1, 0, 2))
    inverse = jnp.pad(inverse, ((0, 0), (0, lanes - tall), (0, 0)))
    top = lax.reduce_precision(inverse, 8, 7)
    low = (inverse - top).astype(jnp.bfloat16)
    top = top.astype(jnp.bfloat16)
    weights = jnp.concatenate([top, top, low], axis=1)
    half, quarter = rows // 2, rows // 4
    w0 = weights[:rows]
    w1 = weights[rows : rows + half]
    w2 = weights[rows + half :]
    m0 = jnp.pad(shifted[:rows], ((0, 0), (0, lanes - comp), (0, lanes - comp)))
    down0, up0 = aggregation_tables(fine_ids)
    down1, up1 = aggregation_tables(coarse_ids)
    rhs = jnp.pad(jnp.transpose(right_side, (1, 2, 0)), ((0, 0), (0, 0), (0, lanes - comp)))

    def field(scale, edged):
        if edged:
            return pltpu.VMEM(
                (rows // scale + 2, cols // scale + 2 * EDGE, lanes), jnp.float32
            )
        return pltpu.VMEM((rows // scale, cols // scale, lanes), jnp.float32)

    vmem = pl.BlockSpec(memory_space=pltpu.VMEM)
    smem = pl.BlockSpec(memory_space=pltpu.SMEM)
    shape = jax.ShapeDtypeStruct(rhs.shape, jnp.float32)
    sol, res = pl.pallas_call(
        functools.partial(cycle_kernel, nlat, nlon),
        out_shape=(shape, shape),
        in_specs=[vmem] * 5 + [smem] * 3 + [vmem] * 4,
        out_specs=(vmem, vmem),
        scratch_shapes=[
            field(1, True), field(1, True), field(2, True), field(2, True),
            field(4, True), field(4, True),
            field(1, False), field(1, False),
            field(2, False), field(2, False), field(2, False),
            field(4, False), field(4, False),
            pltpu.VMEM((2, 2, cols, lanes), jnp.float32),
            pltpu.VMEM((2, 2, rows, lanes), jnp.float32),
            pltpu.VMEM((2, 2, rows, lanes), jnp.float32),
            pltpu.SemaphoreType.DMA((2, 4)),
            pltpu.SemaphoreType.DMA((2, 4)),
        ],
        compiler_params=pltpu.CompilerParams(
            collective_id=0, has_side_effects=True, vmem_limit_bytes=48 * 1024 * 1024
        ),
        name="cycles",
    )(rhs, w0, w1, w2, m0, kappa, kappa1, kappa2, down0, up0, down1, up1)
    return tuple(jnp.transpose(v[:, :, :comp], (2, 0, 1)) for v in (sol, res))


def solution(mesh):
    in_specs = (
        P(None, "lat", "lon"),
        P("lat", None, None),
        P("lat"),
        P("lat", "lon"),
        P("lat", "lon"),
    )
    out_specs = (P(None, "lat", "lon"), P(None, "lat", "lon"))
    return jax.shard_map(
        functools.partial(per_device, mesh.shape["lat"], mesh.shape["lon"]),
        mesh=mesh, in_specs=in_specs, out_specs=out_specs, check_vma=False,
    )
```

```python
import functools

import jax
import jax.numpy as jnp
from jax import lax
from jax.experimental import pallas as pl
from jax.experimental.pallas import tpu as pltpu
from jax.sharding import PartitionSpec as P

SWEEPS = 2
COARSE_SWEEPS = 4
CYCLES = 2
OMEGA = 0.8
SMOOTH_WEIGHT = 2.0 / 3.0
HIGH = lax.Precision.HIGHEST
EDGE = 8


def invert_kernel(width, m_ref, out_ref):
    rows, count, lanes = m_ref.shape
    out_ref[...] = m_ref[...]
    lane = lax.broadcasted_iota(jnp.int32, (count, lanes), 1)

    def step(k, carry):
        at = lane == k
        index = jnp.full((count, lanes), k, jnp.int32)
        row = out_ref[k]
        inv = 1.0 / jnp.take_along_axis(row, index, axis=1)
        row = jnp.where(at, inv, row * inv)
        for i in range(rows):
            mat = out_ref[i]
            col = jnp.take_along_axis(mat, index, axis=1)
            out_ref[i] = jnp.where(at, 0.0, mat) - col * row
        out_ref[k] = row
        return carry

    lax.fori_loop(0, width, step, 0)


def invert_stack(mats, width):
    return pl.pallas_call(
        functools.partial(invert_kernel, width),
        out_shape=jax.ShapeDtypeStruct(mats.shape, jnp.float32),
        in_specs=[pl.BlockSpec(memory_space=pltpu.VMEM)],
        out_specs=pl.BlockSpec(memory_space=pltpu.VMEM),
        compiler_params=pltpu.CompilerParams(vmem_limit_bytes=32 * 1024 * 1024),
        name="invert",
    )(mats)


def cycle_kernel(
    nlat, nlon, rhs, w0, w1, w2, m0, k0, k1, k2, down0, up0, down1, up1,
    sol, res, va, vb, va1, vb1, va2, vb2, x0, r0, b1, x1, r1, x2, r2,
    lat_recv, lon_send, lon_recv, send_sem, recv_sem,
):
    lat = lax.axis_index("lat")
    lon = lax.axis_index("lon")
    west = lax.rem(lon + nlon - 1, nlon)
    east = lax.rem(lon + 1, nlon)
    has_north = lat > 0
    has_south = lat < nlat - 1
    rows, cols, lanes = rhs.shape

    lat_recv[...] = jnp.zeros_like(lat_recv)
    lon_send[...] = jnp.zeros_like(lon_send)

    barrier = pltpu.get_barrier_semaphore()
    for side in (west, east):
        pl.semaphore_signal(
            barrier, inc=1, device_id=(lat, side), device_id_type=pl.DeviceIdType.MESH
        )

    @pl.when(has_north)
    def _():
        pl.semaphore_signal(
            barrier, inc=1, device_id=(lat - 1, lon), device_id_type=pl.DeviceIdType.MESH
        )

    @pl.when(has_south)
    def _():
        pl.semaphore_signal(
            barrier, inc=1, device_id=(lat + 1, lon), device_id_type=pl.DeviceIdType.MESH
        )

    peers = 2 + jnp.minimum(lat, 1) + jnp.minimum(nlat - 1 - lat, 1)
    pl.semaphore_wait(barrier, peers)

    def run(low, high, body):
        count = high - low
        if count <= 0:
            return
        group = next(g for g in (8, 7, 6, 4, 3, 2, 1) if count % g == 0)

        def some(g, carry):
            for i in range(group):
                body(low + g * group + i)
            return carry

        lax.fori_loop(0, count // group, some, 0)

    def lon_parts(field):
        high = field.shape[0] - 2
        if high % 16 == 0:
            return ((0, high // 2), (high // 2, high // 2))
        return ((0, high),)

    def make(src, dst, par, which, target):
        return pltpu.make_async_remote_copy(
            src_ref=src, dst_ref=dst,
            send_sem=send_sem.at[par, which], recv_sem=recv_sem.at[par, which],
            device_id=target, device_id_type=pl.DeviceIdType.MESH,
        )

    def lat_copies(field, par):
        high = field.shape[0] - 2
        wide = field.shape[1] - 2 * EDGE
        inner = pl.ds(EDGE, wide)
        land = pl.ds(0, wide)
        return (
            make(field.at[1, inner], lat_recv.at[par, 1, land], par, 0, (lat - 1, lon)),
            make(field.at[high, inner], lat_recv.at[par, 0, land], par, 1, (lat + 1, lon)),
        )

    def lon_copies(field, par, part):
        low, count = lon_parts(field)[part]
        at = pl.ds(low, max(count, 8))
        return (
            make(lon_send.at[par, 0, at], lon_recv.at[par, 1, at], par, 2 + 2 * part, (lat, west)),
            make(lon_send.at[par, 1, at], lon_recv.at[par, 0, at], par, 3 + 2 * part, (lat, east)),
        )

    def start_lat(field, par):
        north, south = lat_copies(field, par)
        pl.when(has_north)(north.start)
        pl.when(has_south)(south.start)

    def start_lon(field, par, part):
        for copy in lon_copies(field, par, part):
            copy.start()

    def finish_lat(field, par):
        north, south = lat_copies(field, par)
        high = field.shape[0] - 2
        wide = field.shape[1] - 2 * EDGE

        @pl.when(has_north)
        def _():
            north.wait_send()
            south.wait_recv()

        @pl.when(has_south)
        def _():
            south.wait_send()
            north.wait_recv()

        inner = pl.ds(EDGE, wide)
        field[0, inner] = lat_recv[par, 0, pl.ds(0, wide)]
        field[high + 1, inner] = lat_recv[par, 1, pl.ds(0, wide)]

    def finish_lon(field, par, part):
        low, count = lon_parts(field)[part]
        wide = field.shape[1] - 2 * EDGE
        for copy in lon_copies(field, par, part):
            copy.wait()
        for j in range(low, low + count):
            field[j + 1, pl.ds(EDGE - 1, 1)] = lon_recv[par, 0, pl.ds(j, 1)]
            field[j + 1, pl.ds(EDGE + wide, 1)] = lon_recv[par, 1, pl.ds(j, 1)]

    def stage(count, body, used=None, made=None):
        mid = count // 2
        if used is not None:
            finish_lon(*used, 0)
        run(1, mid, body)
        if used is not None:
            if len(lon_parts(used[0])) == 2:
                finish_lon(*used, 1)
            finish_lat(*used)
        body(0)
        body(count - 1)
        if made is not None:
            start_lat(*made)
            if len(lon_parts(made[0])) == 2:
                start_lon(*made, 0)
        run(mid, count - 1, body)
        if made is not None:
            start_lon(*made, len(lon_parts(made[0])) - 1)

    def put(field, par, j, value):
        wide = value.shape[0]
        field[j + 1, pl.ds(EDGE, wide)] = value
        lon_send[par, 0, pl.ds(j, 1)] = value[:1]
        lon_send[par, 1, pl.ds(j, 1)] = value[wide - 1 :]

    def beside(field, kap, j):
        wide = field.shape[1] - 2 * EDGE
        inner = pl.ds(EDGE, wide)
        total = field[j, inner] + field[j + 2, inner]
        total += field[j + 1, pl.ds(EDGE - 1, wide)] + field[j + 1, pl.ds(EDGE + 1, wide)]
        return kap[j] * total

    def split(value):
        top = value.astype(jnp.bfloat16)
        return top, (value - top.astype(jnp.float32)).astype(jnp.bfloat16)

    def solve(weights, j, value):
        top, low = split(value)
        return jnp.dot(
            jnp.concatenate([top, low, top], axis=1), weights[j],
            preferred_element_type=jnp.float32,
        )

    def select(table, value):
        top, low = split(value)
        return jnp.dot(table, top, preferred_element_type=jnp.float32) + jnp.dot(
            table, low, preferred_element_type=jnp.float32
        )

    res[...] = rhs[...]
    sol[...] = jnp.zeros_like(sol)

    def cycle(_, carry):
        def first(j):
            d = OMEGA * solve(w0, j, res[j])
            x0[j] = d
            put(va, 0, j, d)

        stage(rows, first, None, (va, 0))

        def second(j):
            r = (1.0 - OMEGA) * res[j] + beside(va, k0, j)
            r0[j] = r
            d = OMEGA * solve(w0, j, r)
            x0[j] = x0[j] + d
            put(vb, 1, j, d)

        stage(rows, second, (va, 0), (vb, 1))

        def third(j):
            r = (1.0 - OMEGA) * r0[j] + beside(vb, k0, j)
            r0[j] = r
            put(va, 0, j, solve(w0, j, r))

        stage(rows, third, (vb, 1), (va, 0))

        def fourth(p):
            q = [
                (1.0 - SMOOTH_WEIGHT) * r0[2 * p + i]
                + SMOOTH_WEIGHT * beside(va, k0, 2 * p + i)
                for i in range(2)
            ]
            b = select(down0[p], jnp.concatenate(q, axis=0))
            b1[p] = b
            d = OMEGA * solve(w1, p, b)
            x1[p] = d
            put(va1, 1, p, d)

        stage(rows // 2, fourth, (va, 0), (va1, 1))

        def fifth(j):
            r = (1.0 - OMEGA) * b1[j] + beside(va1, k1, j)
            r1[j] = r
            d = OMEGA * solve(w1, j, r)
            x1[j] = x1[j] + d
            put(vb1, 0, j, d)

        stage(rows // 2, fifth, (va1, 1), (vb1, 0))

        def sixth(p):
            q = [
                (1.0 - OMEGA) * r1[2 * p + i] + beside(vb1, k1, 2 * p + i)
                for i in range(2)
            ]
            b = select(down1[p], jnp.concatenate(q, axis=0))
            r2[p] = b
            d = OMEGA * solve(w2, p, b)
            x2[p] = d
            put(va2, 1, p, d)

        stage(rows // 4, sixth, (vb1, 0), (va2, 1))

        here, there, par = va2, vb2, 0
        for sweep in range(1, COARSE_SWEEPS):
            last = sweep == COARSE_SWEEPS - 1

            def coarse(j, here=here, there=there, par=par, last=last):
                r = (1.0 - OMEGA) * r2[j] + beside(here, k2, j)
                r2[j] = r
                d = OMEGA * solve(w2, j, r)
                x2[j] = x2[j] + d
                if not last:
                    put(there, par, j, d)

            made = None if last else (there, par)
            stage(rows // 4, coarse, (here, 1 - par), made)
            here, there, par = there, here, 1 - par

        def seventh(p):
            wide = x1.shape[1]
            up = select(up1[p], x2[p])
            for i in range(2):
                x = x1[2 * p + i] + up[i * wide : (i + 1) * wide]
                x1[2 * p + i] = x
                put(va1, 0, 2 * p + i, x)

        stage(rows // 4, seventh, None, (va1, 0))

        def eighth(j):
            x = (1.0 - OMEGA) * x1[j] + OMEGA * solve(w1, j, b1[j] + beside(va1, k1, j))
            x1[j] = x
            put(vb1, 1, j, x)

        stage(rows // 2, eighth, (va1, 0), (vb1, 1))

        def ninth(p):
            x = (1.0 - OMEGA) * x1[p] + OMEGA * solve(w1, p, b1[p] + beside(vb1, k1, p))
            up = select(up0[p], x)
            for i in range(2):
                put(vb, 0, 2 * p + i, up[i * cols : (i + 1) * cols])

        stage(rows // 2, ninth, (vb1, 1), (vb, 0))

        def tenth(j):
            e = vb[j + 1, pl.ds(EDGE, cols)]
            x = x0[j] + (1.0 - SMOOTH_WEIGHT) * e
            x += SMOOTH_WEIGHT * solve(w0, j, beside(vb, k0, j))
            x0[j] = x
            put(va, 1, j, x)

        stage(rows, tenth, (vb, 0), (va, 1))

        def eleventh(j):
            x = (1.0 - OMEGA) * x0[j] + OMEGA * solve(w0, j, res[j] + beside(va, k0, j))
            x0[j] = x
            put(vb, 0, j, x)

        stage(rows, eleventh, (va, 1), (vb, 0))

        def twelfth(j):
            x = (1.0 - OMEGA) * x0[j] + OMEGA * solve(w0, j, res[j] + beside(vb, k0, j))
            x0[j] = x
            sol[j] = sol[j] + x
            put(va, 1, j, x)

        stage(rows, twelfth, (vb, 0), (va, 1))

        def product(j):
            res[j] = res[j] - jnp.dot(
                x0[j], m0[j], precision=HIGH, preferred_element_type=jnp.float32
            )

        run(0, rows, product)

        def remainder(j):
            res[j] = res[j] + beside(va, k0, j)

        stage(rows, remainder, (va, 1))
        return carry

    lax.fori_loop(0, CYCLES, cycle, 0)


def coarsen_tables(blocks, kappa):
    rows = blocks.shape[0] // 2
    grouped = blocks.reshape(rows, 2, blocks.shape[1], blocks.shape[2])
    return (4.0 * jnp.mean(grouped, axis=1), 2.0 * jnp.mean(kappa.reshape(rows, 2), axis=1))


def aggregation_tables(ids):
    rows, cols = ids.shape
    flat = ids.reshape(rows // 2, 2 * cols)
    targets = jnp.arange(cols // 2, dtype=jnp.int32)
    down = (flat[:, None, :] == targets[None, :, None]).astype(jnp.bfloat16)
    up = (flat[:, :, None] == targets).astype(jnp.bfloat16)
    return down, up


def per_device(nlat, nlon, right_side, blocks, kappa, fine_ids, coarse_ids):
    comp, rows, cols = right_side.shape
    lanes = -(-comp // 128) * 128
    tall = -(-comp // 8) * 8
    blocks1, kappa1 = coarsen_tables(blocks, kappa)
    blocks2, kappa2 = coarsen_tables(blocks1, kappa1)
    eye = jnp.eye(comp, dtype=jnp.float32)
    shifted = jnp.concatenate(
        [
            b + 4.0 * k[:, None, None] * eye
            for b, k in ((blocks, kappa), (blocks1, kappa1), (blocks2, kappa2))
        ],
        axis=0,
    )
    total = shifted.shape[0]
    batch = -(-total // 8) * 8
    filler = jnp.broadcast_to(eye, (batch - total, comp, comp))
    stacked = jnp.transpose(jnp.concatenate([shifted, filler], axis=0), (1, 0, 2))
    stacked = jnp.pad(stacked, ((0, tall - comp), (0, 0), (0, lanes - comp)))
    inverse = jnp.transpose(invert_stack(stacked, comp)[:, :total], (1, 0, 2))
    inverse = jnp.pad(inverse, ((0, 0), (0, lanes - tall), (0, 0)))
    top = lax.reduce_precision(inverse, 8, 7)
    low = (inverse - top).astype(jnp.bfloat16)
    top = top.astype(jnp.bfloat16)
    weights = jnp.concatenate([top, top, low], axis=1)
    half, quarter = rows // 2, rows // 4
    w0 = weights[:rows]
    w1 = weights[rows : rows + half]
    w2 = weights[rows + half :]
    m0 = jnp.pad(shifted[:rows], ((0, 0), (0, lanes - comp), (0, lanes - comp)))
    down0, up0 = aggregation_tables(fine_ids)
    down1, up1 = aggregation_tables(coarse_ids)
    rhs = jnp.pad(jnp.transpose(right_side, (1, 2, 0)), ((0, 0), (0, 0), (0, lanes - comp)))

    def field(scale, edged):
        if edged:
            return pltpu.VMEM(
                (rows // scale + 2, cols // scale + 2 * EDGE, lanes), jnp.float32
            )
        return pltpu.VMEM((rows // scale, cols // scale, lanes), jnp.float32)

    vmem = pl.BlockSpec(memory_space=pltpu.VMEM)
    smem = pl.BlockSpec(memory_space=pltpu.SMEM)
    shape = jax.ShapeDtypeStruct(rhs.shape, jnp.float32)
    sol, res = pl.pallas_call(
        functools.partial(cycle_kernel, nlat, nlon),
        out_shape=(shape, shape),
        in_specs=[vmem] * 5 + [smem] * 3 + [vmem] * 4,
        out_specs=(vmem, vmem),
        scratch_shapes=[
            field(1, True), field(1, True), field(2, True), field(2, True),
            field(4, True), field(4, True),
            field(1, False), field(1, False),
            field(2, False), field(2, False), field(2, False),
            field(4, False), field(4, False),
            pltpu.VMEM((2, 2, cols, lanes), jnp.float32),
            pltpu.VMEM((2, 2, rows, lanes), jnp.float32),
            pltpu.VMEM((2, 2, rows, lanes), jnp.float32),
            pltpu.SemaphoreType.DMA((2, 6)),
            pltpu.SemaphoreType.DMA((2, 6)),
        ],
        compiler_params=pltpu.CompilerParams(
            collective_id=0, has_side_effects=True, vmem_limit_bytes=48 * 1024 * 1024
        ),
        name="cycles",
    )(rhs, w0, w1, w2, m0, kappa, kappa1, kappa2, down0, up0, down1, up1)
    return tuple(jnp.transpose(v[:, :, :comp], (2, 0, 1)) for v in (sol, res))


def solution(mesh):
    in_specs = (
        P(None, "lat", "lon"),
        P("lat", None, None),
        P("lat"),
        P("lat", "lon"),
        P("lat", "lon"),
    )
    out_specs = (P(None, "lat", "lon"), P(None, "lat", "lon"))
    return jax.shard_map(
        functools.partial(per_device, mesh.shape["lat"], mesh.shape["lon"]),
        mesh=mesh, in_specs=in_specs, out_specs=out_specs, check_vma=False,
    )
```

```python
import functools

import jax
import jax.numpy as jnp
from jax import lax
from jax.experimental import pallas as pl
from jax.experimental.pallas import tpu as pltpu
from jax.sharding import PartitionSpec as P

SWEEPS = 2
COARSE_SWEEPS = 4
CYCLES = 2
OMEGA = 0.8
SMOOTH_WEIGHT = 2.0 / 3.0
HIGH = lax.Precision.HIGHEST
EDGE = 8
TEAM = 4


def invert_kernel(width, m_ref, out_ref):
    rows, count, lanes = m_ref.shape
    out_ref[...] = m_ref[...]
    lane = lax.broadcasted_iota(jnp.int32, (count, lanes), 1)

    def step(k, carry):
        at = lane == k
        index = jnp.full((count, lanes), k, jnp.int32)
        row = out_ref[k]
        inv = 1.0 / jnp.take_along_axis(row, index, axis=1)
        row = jnp.where(at, inv, row * inv)
        for i in range(rows):
            mat = out_ref[i]
            col = jnp.take_along_axis(mat, index, axis=1)
            out_ref[i] = jnp.where(at, 0.0, mat) - col * row
        out_ref[k] = row
        return carry

    lax.fori_loop(0, width, step, 0)


def invert_stack(mats, width):
    return pl.pallas_call(
        functools.partial(invert_kernel, width),
        out_shape=jax.ShapeDtypeStruct(mats.shape, jnp.float32),
        in_specs=[pl.BlockSpec(memory_space=pltpu.VMEM)],
        out_specs=pl.BlockSpec(memory_space=pltpu.VMEM),
        compiler_params=pltpu.CompilerParams(vmem_limit_bytes=32 * 1024 * 1024),
        name="invert",
    )(mats)


def cycle_kernel(
    nlat, nlon, rhs, w0, w1, w2, m0, k0, k1, k2, down0, up0, down1, up1,
    sol, res, va, vb, va1, vb1, va2, vb2, x0, r0, b1, x1, r1, x2, r2,
    lat_recv, lon_send, lon_recv, send_sem, recv_sem,
):
    lat = lax.axis_index("lat")
    lon = lax.axis_index("lon")
    west = lax.rem(lon + nlon - 1, nlon)
    east = lax.rem(lon + 1, nlon)
    has_north = lat > 0
    has_south = lat < nlat - 1
    rows, cols, lanes = rhs.shape

    lat_recv[...] = jnp.zeros_like(lat_recv)
    lon_send[...] = jnp.zeros_like(lon_send)

    barrier = pltpu.get_barrier_semaphore()
    for side in (west, east):
        pl.semaphore_signal(
            barrier, inc=1, device_id=(lat, side), device_id_type=pl.DeviceIdType.MESH
        )

    @pl.when(has_north)
    def _():
        pl.semaphore_signal(
            barrier, inc=1, device_id=(lat - 1, lon), device_id_type=pl.DeviceIdType.MESH
        )

    @pl.when(has_south)
    def _():
        pl.semaphore_signal(
            barrier, inc=1, device_id=(lat + 1, lon), device_id_type=pl.DeviceIdType.MESH
        )

    peers = 2 + jnp.minimum(lat, 1) + jnp.minimum(nlat - 1 - lat, 1)
    pl.semaphore_wait(barrier, peers)

    def run(low, high, body):
        count = high - low
        if count <= 0:
            return
        group = next(g for g in (8, 7, 6, 4, 3, 2, 1) if count % g == 0)

        def some(g, carry):
            for i in range(group):
                body(low + g * group + i)
            return carry

        lax.fori_loop(0, count // group, some, 0)

    def lon_parts(field):
        high = field.shape[0] - 2
        if high % 16 == 0:
            return ((0, high // 2), (high // 2, high // 2))
        return ((0, high),)

    def make(src, dst, par, which, target):
        return pltpu.make_async_remote_copy(
            src_ref=src, dst_ref=dst,
            send_sem=send_sem.at[par, which], recv_sem=recv_sem.at[par, which],
            device_id=target, device_id_type=pl.DeviceIdType.MESH,
        )

    def lat_copies(field, par):
        high = field.shape[0] - 2
        wide = field.shape[1] - 2 * EDGE
        inner = pl.ds(EDGE, wide)
        land = pl.ds(0, wide)
        return (
            make(field.at[1, inner], lat_recv.at[par, 1, land], par, 0, (lat - 1, lon)),
            make(field.at[high, inner], lat_recv.at[par, 0, land], par, 1, (lat + 1, lon)),
        )

    def lon_copies(field, par, part):
        low, count = lon_parts(field)[part]
        at = pl.ds(low, max(count, 8))
        return (
            make(lon_send.at[par, 0, at], lon_recv.at[par, 1, at], par, 2 + 2 * part, (lat, west)),
            make(lon_send.at[par, 1, at], lon_recv.at[par, 0, at], par, 3 + 2 * part, (lat, east)),
        )

    def start_lat(field, par):
        north, south = lat_copies(field, par)
        pl.when(has_north)(north.start)
        pl.when(has_south)(south.start)

    def start_lon(field, par, part):
        for copy in lon_copies(field, par, part):
            copy.start()

    def finish_lat(field, par):
        north, south = lat_copies(field, par)
        high = field.shape[0] - 2
        wide = field.shape[1] - 2 * EDGE

        @pl.when(has_north)
        def _():
            north.wait_send()
            south.wait_recv()

        @pl.when(has_south)
        def _():
            south.wait_send()
            north.wait_recv()

        inner = pl.ds(EDGE, wide)
        field[0, inner] = lat_recv[par, 0, pl.ds(0, wide)]
        field[high + 1, inner] = lat_recv[par, 1, pl.ds(0, wide)]

    def finish_lon(field, par, part):
        low, count = lon_parts(field)[part]
        wide = field.shape[1] - 2 * EDGE
        for copy in lon_copies(field, par, part):
            copy.wait()
        for j in range(low, low + count):
            field[j + 1, pl.ds(EDGE - 1, 1)] = lon_recv[par, 0, pl.ds(j, 1)]
            field[j + 1, pl.ds(EDGE + wide, 1)] = lon_recv[par, 1, pl.ds(j, 1)]

    def stage(count, body, used=None, made=None):
        mid = count // 2
        if used is not None:
            finish_lon(*used, 0)
        run(1, mid, body)
        if used is not None:
            if len(lon_parts(used[0])) == 2:
                finish_lon(*used, 1)
            finish_lat(*used)
        body(0)
        body(count - 1)
        if made is not None:
            start_lat(*made)
            if len(lon_parts(made[0])) == 2:
                start_lon(*made, 0)
        run(mid, count - 1, body)
        if made is not None:
            start_lon(*made, len(lon_parts(made[0])) - 1)

    def put(field, par, j, value):
        wide = value.shape[0]
        field[j + 1, pl.ds(EDGE, wide)] = value
        lon_send[par, 0, pl.ds(j, 1)] = value[:1]
        lon_send[par, 1, pl.ds(j, 1)] = value[wide - 1 :]

    def beside(field, kap, j):
        wide = field.shape[1] - 2 * EDGE
        inner = pl.ds(EDGE, wide)
        total = field[j, inner] + field[j + 2, inner]
        total += field[j + 1, pl.ds(EDGE - 1, wide)] + field[j + 1, pl.ds(EDGE + 1, wide)]
        return kap[j] * total

    def split(value):
        top = value.astype(jnp.bfloat16)
        return top, (value - top.astype(jnp.float32)).astype(jnp.bfloat16)

    def solve(weights, j, value):
        top, low = split(value)
        return jnp.dot(
            jnp.concatenate([top, low, top], axis=1), weights[j],
            preferred_element_type=jnp.float32,
        )

    def select(table, value):
        top, low = split(value)
        return jnp.dot(table, top, preferred_element_type=jnp.float32) + jnp.dot(
            table, low, preferred_element_type=jnp.float32
        )

    res[...] = rhs[...]
    sol[...] = jnp.zeros_like(sol)

    def cycle(_, carry):
        def first(j):
            d = OMEGA * solve(w0, j, res[j])
            x0[j] = d
            put(va, 0, j, d)

        stage(rows, first, None, (va, 0))

        def second(j):
            r = (1.0 - OMEGA) * res[j] + beside(va, k0, j)
            r0[j] = r
            d = OMEGA * solve(w0, j, r)
            x0[j] = x0[j] + d
            put(vb, 1, j, d)

        stage(rows, second, (va, 0), (vb, 1))

        def third(j):
            r = (1.0 - OMEGA) * r0[j] + beside(vb, k0, j)
            r0[j] = r
            put(va, 0, j, solve(w0, j, r))

        stage(rows, third, (vb, 1), (va, 0))

        def fourth(p):
            q = [
                (1.0 - SMOOTH_WEIGHT) * r0[2 * p + i]
                + SMOOTH_WEIGHT * beside(va, k0, 2 * p + i)
                for i in range(2)
            ]
            b = select(down0[p], jnp.concatenate(q, axis=0))
            b1[p] = b
            d = OMEGA * solve(w1, p, b)
            x1[p] = d
            put(va1, 1, p, d)

        stage(rows // 2, fourth, (va, 0), (va1, 1))

        def fifth(j):
            r = (1.0 - OMEGA) * b1[j] + beside(va1, k1, j)
            r1[j] = r
            d = OMEGA * solve(w1, j, r)
            x1[j] = x1[j] + d
            put(vb1, 0, j, d)

        stage(rows // 2, fifth, (va1, 1), (vb1, 0))

        def sixth(p):
            q = [
                (1.0 - OMEGA) * r1[2 * p + i] + beside(vb1, k1, 2 * p + i)
                for i in range(2)
            ]
            b = select(down1[p], jnp.concatenate(q, axis=0))
            r2[p] = b
            d = OMEGA * solve(w2, p, b)
            x2[p] = d
            put(va2, 1, p, d)

        stage(rows // 4, sixth, (vb1, 0), (va2, 1))

        here, there, par = va2, vb2, 0
        for sweep in range(1, COARSE_SWEEPS):
            last = sweep == COARSE_SWEEPS - 1

            def coarse(j, here=here, there=there, par=par, last=last):
                r = (1.0 - OMEGA) * r2[j] + beside(here, k2, j)
                r2[j] = r
                d = OMEGA * solve(w2, j, r)
                x2[j] = x2[j] + d
                if not last:
                    put(there, par, j, d)

            made = None if last else (there, par)
            stage(rows // 4, coarse, (here, 1 - par), made)
            here, there, par = there, here, 1 - par

        def seventh(p):
            wide = x1.shape[1]
            up = select(up1[p], x2[p])
            for i in range(2):
                x = x1[2 * p + i] + up[i * wide : (i + 1) * wide]
                x1[2 * p + i] = x
                put(va1, 0, 2 * p + i, x)

        stage(rows // 4, seventh, None, (va1, 0))

        def eighth(j):
            x = (1.0 - OMEGA) * x1[j] + OMEGA * solve(w1, j, b1[j] + beside(va1, k1, j))
            x1[j] = x
            put(vb1, 1, j, x)

        stage(rows // 2, eighth, (va1, 0), (vb1, 1))

        def ninth(p):
            x = (1.0 - OMEGA) * x1[p] + OMEGA * solve(w1, p, b1[p] + beside(vb1, k1, p))
            up = select(up0[p], x)
            for i in range(2):
                put(vb, 0, 2 * p + i, up[i * cols : (i + 1) * cols])

        stage(rows // 2, ninth, (vb1, 1), (vb, 0))

        def tenth(j):
            e = vb[j + 1, pl.ds(EDGE, cols)]
            x = x0[j] + (1.0 - SMOOTH_WEIGHT) * e
            x += SMOOTH_WEIGHT * solve(w0, j, beside(vb, k0, j))
            x0[j] = x
            put(va, 1, j, x)

        stage(rows, tenth, (vb, 0), (va, 1))

        def eleventh(j):
            x = (1.0 - OMEGA) * x0[j] + OMEGA * solve(w0, j, res[j] + beside(va, k0, j))
            x0[j] = x
            put(vb, 0, j, x)

        stage(rows, eleventh, (va, 1), (vb, 0))

        def twelfth(j):
            x = (1.0 - OMEGA) * x0[j] + OMEGA * solve(w0, j, res[j] + beside(vb, k0, j))
            x0[j] = x
            sol[j] = sol[j] + x
            put(va, 1, j, x)

        stage(rows, twelfth, (vb, 0), (va, 1))

        def product(j):
            res[j] = res[j] - jnp.dot(
                x0[j], m0[j], precision=HIGH, preferred_element_type=jnp.float32
            )

        run(0, rows, product)

        def remainder(j):
            res[j] = res[j] + beside(va, k0, j)

        stage(rows, remainder, (va, 1))
        return carry

    lax.fori_loop(0, CYCLES, cycle, 0)


def coarsen_tables(blocks, kappa):
    rows = blocks.shape[0] // 2
    grouped = blocks.reshape(rows, 2, blocks.shape[1], blocks.shape[2])
    return (4.0 * jnp.mean(grouped, axis=1), 2.0 * jnp.mean(kappa.reshape(rows, 2), axis=1))


def aggregation_tables(ids):
    rows, cols = ids.shape
    flat = ids.reshape(rows // 2, 2 * cols)
    targets = jnp.arange(cols // 2, dtype=jnp.int32)
    down = (flat[:, None, :] == targets[None, :, None]).astype(jnp.bfloat16)
    up = (flat[:, :, None] == targets).astype(jnp.bfloat16)
    return down, up


def per_device(nlat, nlon, right_side, blocks, kappa, fine_ids, coarse_ids):
    comp, rows, cols = right_side.shape
    lanes = -(-comp // 128) * 128
    tall = -(-comp // 8) * 8
    blocks1, kappa1 = coarsen_tables(blocks, kappa)
    blocks2, kappa2 = coarsen_tables(blocks1, kappa1)
    eye = jnp.eye(comp, dtype=jnp.float32)
    shifted = jnp.concatenate(
        [
            b + 4.0 * k[:, None, None] * eye
            for b, k in ((blocks, kappa), (blocks1, kappa1), (blocks2, kappa2))
        ],
        axis=0,
    )
    total = shifted.shape[0]
    team = TEAM if nlon % TEAM == 0 else 1
    share = -(-total // team)
    batch = -(-share // 8) * 8
    filler = jnp.broadcast_to(eye, (share * (team - 1) + batch - total, comp, comp))
    member = lax.rem(lax.axis_index("lon"), team)
    mine = lax.dynamic_slice_in_dim(
        jnp.concatenate([shifted, filler], axis=0), member * share, batch, axis=0
    )
    stacked = jnp.transpose(mine, (1, 0, 2))
    stacked = jnp.pad(stacked, ((0, tall - comp), (0, 0), (0, lanes - comp)))
    mine = jnp.transpose(invert_stack(stacked, comp)[:, :share], (1, 0, 2))
    teams = [[i + j for j in range(team)] for i in range(0, nlon, team)]
    inverse = lax.all_gather(mine, "lon", axis_index_groups=teams, axis=0, tiled=True)[:total]
    inverse = jnp.pad(inverse, ((0, 0), (0, lanes - tall), (0, 0)))
    top = lax.reduce_precision(inverse, 8, 7)
    low = (inverse - top).astype(jnp.bfloat16)
    top = top.astype(jnp.bfloat16)
    weights = jnp.concatenate([top, top, low], axis=1)
    half, quarter = rows // 2, rows // 4
    w0 = weights[:rows]
    w1 = weights[rows : rows + half]
    w2 = weights[rows + half :]
    m0 = jnp.pad(shifted[:rows], ((0, 0), (0, lanes - comp), (0, lanes - comp)))
    down0, up0 = aggregation_tables(fine_ids)
    down1, up1 = aggregation_tables(coarse_ids)
    rhs = jnp.pad(jnp.transpose(right_side, (1, 2, 0)), ((0, 0), (0, 0), (0, lanes - comp)))

    def field(scale, edged):
        if edged:
            return pltpu.VMEM(
                (rows // scale + 2, cols // scale + 2 * EDGE, lanes), jnp.float32
            )
        return pltpu.VMEM((rows // scale, cols // scale, lanes), jnp.float32)

    vmem = pl.BlockSpec(memory_space=pltpu.VMEM)
    smem = pl.BlockSpec(memory_space=pltpu.SMEM)
    shape = jax.ShapeDtypeStruct(rhs.shape, jnp.float32)
    sol, res = pl.pallas_call(
        functools.partial(cycle_kernel, nlat, nlon),
        out_shape=(shape, shape),
        in_specs=[vmem] * 5 + [smem] * 3 + [vmem] * 4,
        out_specs=(vmem, vmem),
        scratch_shapes=[
            field(1, True), field(1, True), field(2, True), field(2, True),
            field(4, True), field(4, True),
            field(1, False), field(1, False),
            field(2, False), field(2, False), field(2, False),
            field(4, False), field(4, False),
            pltpu.VMEM((2, 2, cols, lanes), jnp.float32),
            pltpu.VMEM((2, 2, rows, lanes), jnp.float32),
            pltpu.VMEM((2, 2, rows, lanes), jnp.float32),
            pltpu.SemaphoreType.DMA((2, 6)),
            pltpu.SemaphoreType.DMA((2, 6)),
        ],
        compiler_params=pltpu.CompilerParams(
            collective_id=0, has_side_effects=True, vmem_limit_bytes=48 * 1024 * 1024
        ),
        name="cycles",
    )(rhs, w0, w1, w2, m0, kappa, kappa1, kappa2, down0, up0, down1, up1)
    return tuple(jnp.transpose(v[:, :, :comp], (2, 0, 1)) for v in (sol, res))


def solution(mesh):
    in_specs = (
        P(None, "lat", "lon"),
        P("lat", None, None),
        P("lat"),
        P("lat", "lon"),
        P("lat", "lon"),
    )
    out_specs = (P(None, "lat", "lon"), P(None, "lat", "lon"))
    return jax.shard_map(
        functools.partial(per_device, mesh.shape["lat"], mesh.shape["lon"]),
        mesh=mesh, in_specs=in_specs, out_specs=out_specs, check_vma=False,
    )
```

```python
import functools

import jax
import jax.numpy as jnp
from jax import lax
from jax.experimental import pallas as pl
from jax.experimental.pallas import tpu as pltpu
from jax.sharding import PartitionSpec as P

SWEEPS = 2
COARSE_SWEEPS = 4
CYCLES = 2
OMEGA = 0.8
SMOOTH_WEIGHT = 2.0 / 3.0
HIGH = lax.Precision.HIGHEST
EDGE = 8
TEAM = 4


def invert_kernel(width, m_ref, out_ref):
    rows, count, lanes = m_ref.shape
    out_ref[...] = m_ref[...]
    lane = lax.broadcasted_iota(jnp.int32, (count, lanes), 1)

    def step(k, carry):
        at = lane == k
        index = jnp.full((count, lanes), k, jnp.int32)
        row = out_ref[k]
        inv = 1.0 / jnp.take_along_axis(row, index, axis=1)
        row = jnp.where(at, inv, row * inv)
        for i in range(rows):
            mat = out_ref[i]
            col = jnp.take_along_axis(mat, index, axis=1)
            out_ref[i] = jnp.where(at, 0.0, mat) - col * row
        out_ref[k] = row
        return carry

    lax.fori_loop(0, width, step, 0)


def invert_stack(mats, width):
    return pl.pallas_call(
        functools.partial(invert_kernel, width),
        out_shape=jax.ShapeDtypeStruct(mats.shape, jnp.float32),
        in_specs=[pl.BlockSpec(memory_space=pltpu.VMEM)],
        out_specs=pl.BlockSpec(memory_space=pltpu.VMEM),
        compiler_params=pltpu.CompilerParams(vmem_limit_bytes=32 * 1024 * 1024),
        name="invert",
    )(mats)


def cycle_kernel(
    nlat, nlon, rhs, w0, w1, w2, m0, k0, k1, k2, down0, up0, down1, up1,
    sol, res, va, vb, va1, vb1, va2, vb2, x0, r0, b1, x1, r1, x2, r2,
    lat_recv, lon_send, lon_recv, send_sem, recv_sem,
):
    lat = lax.axis_index("lat")
    lon = lax.axis_index("lon")
    west = lax.rem(lon + nlon - 1, nlon)
    east = lax.rem(lon + 1, nlon)
    has_north = lat > 0
    has_south = lat < nlat - 1
    rows, cols, lanes = rhs.shape

    lat_recv[...] = jnp.zeros_like(lat_recv)
    lon_send[...] = jnp.zeros_like(lon_send)

    barrier = pltpu.get_barrier_semaphore()
    for side in (west, east):
        pl.semaphore_signal(
            barrier, inc=1, device_id=(lat, side), device_id_type=pl.DeviceIdType.MESH
        )

    @pl.when(has_north)
    def _():
        pl.semaphore_signal(
            barrier, inc=1, device_id=(lat - 1, lon), device_id_type=pl.DeviceIdType.MESH
        )

    @pl.when(has_south)
    def _():
        pl.semaphore_signal(
            barrier, inc=1, device_id=(lat + 1, lon), device_id_type=pl.DeviceIdType.MESH
        )

    peers = 2 + jnp.minimum(lat, 1) + jnp.minimum(nlat - 1 - lat, 1)
    pl.semaphore_wait(barrier, peers)

    def run(low, high, body):
        count = high - low
        if count <= 0:
            return
        group = next(g for g in (8, 7, 6, 4, 3, 2, 1) if count % g == 0)

        def some(g, carry):
            for i in range(group):
                body(low + g * group + i)
            return carry

        lax.fori_loop(0, count // group, some, 0)

    def lon_parts(field):
        high = field.shape[0] - 2
        if high % 16 == 0:
            return ((0, high // 2), (high // 2, high // 2))
        return ((0, high),)

    def make(src, dst, par, which, target):
        return pltpu.make_async_remote_copy(
            src_ref=src, dst_ref=dst,
            send_sem=send_sem.at[par, which], recv_sem=recv_sem.at[par, which],
            device_id=target, device_id_type=pl.DeviceIdType.MESH,
        )

    def lat_copies(field, par):
        high = field.shape[0] - 2
        wide = field.shape[1] - 2 * EDGE
        inner = pl.ds(EDGE, wide)
        land = pl.ds(0, wide)
        return (
            make(field.at[1, inner], lat_recv.at[par, 1, land], par, 0, (lat - 1, lon)),
            make(field.at[high, inner], lat_recv.at[par, 0, land], par, 1, (lat + 1, lon)),
        )

    def lon_copies(field, par, part):
        low, count = lon_parts(field)[part]
        at = pl.ds(low, max(count, 8))
        return (
            make(lon_send.at[par, 0, at], lon_recv.at[par, 1, at], par, 2 + 2 * part, (lat, west)),
            make(lon_send.at[par, 1, at], lon_recv.at[par, 0, at], par, 3 + 2 * part, (lat, east)),
        )

    def start_lat(field, par):
        north, south = lat_copies(field, par)
        pl.when(has_north)(north.start)
        pl.when(has_south)(south.start)

    def start_lon(field, par, part):
        for copy in lon_copies(field, par, part):
            copy.start()

    def finish_lat(field, par):
        north, south = lat_copies(field, par)
        high = field.shape[0] - 2
        wide = field.shape[1] - 2 * EDGE

        @pl.when(has_north)
        def _():
            north.wait_send()
            south.wait_recv()

        @pl.when(has_south)
        def _():
            south.wait_send()
            north.wait_recv()

        inner = pl.ds(EDGE, wide)
        field[0, inner] = lat_recv[par, 0, pl.ds(0, wide)]
        field[high + 1, inner] = lat_recv[par, 1, pl.ds(0, wide)]

    def finish_lon(field, par, part):
        low, count = lon_parts(field)[part]
        wide = field.shape[1] - 2 * EDGE
        for copy in lon_copies(field, par, part):
            copy.wait()
        for j in range(low, low + count):
            field[j + 1, pl.ds(EDGE - 1, 1)] = lon_recv[par, 0, pl.ds(j, 1)]
            field[j + 1, pl.ds(EDGE + wide, 1)] = lon_recv[par, 1, pl.ds(j, 1)]

    def stage(count, body, used=None, made=None):
        mid = count // 2
        if used is not None:
            finish_lon(*used, 0)
        run(1, mid, body)
        if used is not None:
            if len(lon_parts(used[0])) == 2:
                finish_lon(*used, 1)
            finish_lat(*used)
        body(0)
        body(count - 1)
        if made is not None:
            start_lat(*made)
            if len(lon_parts(made[0])) == 2:
                start_lon(*made, 0)
        run(mid, count - 1, body)
        if made is not None:
            start_lon(*made, len(lon_parts(made[0])) - 1)

    def put(field, par, j, value):
        wide = value.shape[0]
        field[j + 1, pl.ds(EDGE, wide)] = value
        lon_send[par, 0, pl.ds(j, 1)] = value[:1]
        lon_send[par, 1, pl.ds(j, 1)] = value[wide - 1 :]

    def beside(field, kap, j):
        wide = field.shape[1] - 2 * EDGE
        inner = pl.ds(EDGE, wide)
        total = field[j, inner] + field[j + 2, inner]
        total += field[j + 1, pl.ds(EDGE - 1, wide)] + field[j + 1, pl.ds(EDGE + 1, wide)]
        return kap[j] * total

    def split(value):
        top = value.astype(jnp.bfloat16)
        return top, (value - top.astype(jnp.float32)).astype(jnp.bfloat16)

    def solve(weights, j, value):
        top, low = split(value)
        return jnp.dot(
            jnp.concatenate([top, low, top], axis=1), weights[j],
            preferred_element_type=jnp.float32,
        )

    def select(table, value):
        top, low = split(value)
        return jnp.dot(table, top, preferred_element_type=jnp.float32) + jnp.dot(
            table, low, preferred_element_type=jnp.float32
        )

    res[...] = rhs[...]
    sol[...] = jnp.zeros_like(sol)

    def cycle(_, carry):
        def first(j):
            d = OMEGA * solve(w0, j, res[j])
            x0[j] = d
            put(va, 0, j, d)

        stage(rows, first, None, (va, 0))

        def second(j):
            r = (1.0 - OMEGA) * res[j] + beside(va, k0, j)
            r0[j] = r
            d = OMEGA * solve(w0, j, r)
            x0[j] = x0[j] + d
            put(vb, 1, j, d)

        stage(rows, second, (va, 0), (vb, 1))

        def third(j):
            r = (1.0 - OMEGA) * r0[j] + beside(vb, k0, j)
            r0[j] = r
            put(va, 0, j, solve(w0, j, r))

        stage(rows, third, (vb, 1), (va, 0))

        def fourth(p):
            q = [
                (1.0 - SMOOTH_WEIGHT) * r0[2 * p + i]
                + SMOOTH_WEIGHT * beside(va, k0, 2 * p + i)
                for i in range(2)
            ]
            b = select(down0[p], jnp.concatenate(q, axis=0))
            b1[p] = b
            d = OMEGA * solve(w1, p, b)
            x1[p] = d
            put(va1, 1, p, d)

        stage(rows // 2, fourth, (va, 0), (va1, 1))

        def fifth(j):
            r = (1.0 - OMEGA) * b1[j] + beside(va1, k1, j)
            r1[j] = r
            d = OMEGA * solve(w1, j, r)
            x1[j] = x1[j] + d
            put(vb1, 0, j, d)

        stage(rows // 2, fifth, (va1, 1), (vb1, 0))

        def sixth(p):
            q = [
                (1.0 - OMEGA) * r1[2 * p + i] + beside(vb1, k1, 2 * p + i)
                for i in range(2)
            ]
            b = select(down1[p], jnp.concatenate(q, axis=0))
            r2[p] = b
            d = OMEGA * solve(w2, p, b)
            x2[p] = d
            put(va2, 1, p, d)

        stage(rows // 4, sixth, (vb1, 0), (va2, 1))

        here, there, par = va2, vb2, 0
        for sweep in range(1, COARSE_SWEEPS):
            last = sweep == COARSE_SWEEPS - 1

            def coarse(j, here=here, there=there, par=par, last=last):
                r = (1.0 - OMEGA) * r2[j] + beside(here, k2, j)
                r2[j] = r
                d = OMEGA * solve(w2, j, r)
                x2[j] = x2[j] + d
                if not last:
                    put(there, par, j, d)

            made = None if last else (there, par)
            stage(rows // 4, coarse, (here, 1 - par), made)
            here, there, par = there, here, 1 - par

        def seventh(p):
            wide = x1.shape[1]
            up = select(up1[p], x2[p])
            for i in range(2):
                x = x1[2 * p + i] + up[i * wide : (i + 1) * wide]
                x1[2 * p + i] = x
                put(va1, 0, 2 * p + i, x)

        stage(rows // 4, seventh, None, (va1, 0))

        def eighth(j):
            x = (1.0 - OMEGA) * x1[j] + OMEGA * solve(w1, j, b1[j] + beside(va1, k1, j))
            x1[j] = x
            put(vb1, 1, j, x)

        stage(rows // 2, eighth, (va1, 0), (vb1, 1))

        def ninth(p):
            x = (1.0 - OMEGA) * x1[p] + OMEGA * solve(w1, p, b1[p] + beside(vb1, k1, p))
            up = select(up0[p], x)
            for i in range(2):
                put(vb, 0, 2 * p + i, up[i * cols : (i + 1) * cols])

        stage(rows // 2, ninth, (vb1, 1), (vb, 0))

        def tenth(j):
            e = vb[j + 1, pl.ds(EDGE, cols)]
            x = x0[j] + (1.0 - SMOOTH_WEIGHT) * e
            x += SMOOTH_WEIGHT * solve(w0, j, beside(vb, k0, j))
            x0[j] = x
            put(va, 1, j, x)

        stage(rows, tenth, (vb, 0), (va, 1))

        def eleventh(j):
            x = (1.0 - OMEGA) * x0[j] + OMEGA * solve(w0, j, res[j] + beside(va, k0, j))
            x0[j] = x
            put(vb, 0, j, x)

        stage(rows, eleventh, (va, 1), (vb, 0))

        def twelfth(j):
            x = (1.0 - OMEGA) * x0[j] + OMEGA * solve(w0, j, res[j] + beside(vb, k0, j))
            x0[j] = x
            sol[j] = sol[j] + x
            put(va, 1, j, x)

        stage(rows, twelfth, (vb, 0), (va, 1))

        def product(j):
            res[j] = res[j] - jnp.dot(
                x0[j], m0[j], precision=HIGH, preferred_element_type=jnp.float32
            )

        run(0, rows, product)

        def remainder(j):
            res[j] = res[j] + beside(va, k0, j)

        stage(rows, remainder, (va, 1))
        return carry

    lax.fori_loop(0, CYCLES, cycle, 0)


def coarsen_tables(blocks, kappa):
    rows = blocks.shape[0] // 2
    grouped = blocks.reshape(rows, 2, blocks.shape[1], blocks.shape[2])
    pairs = kappa.reshape(rows, 2)
    return (2.0 * (grouped[:, 0] + grouped[:, 1]), pairs[:, 0] + pairs[:, 1])


def aggregation_tables(ids):
    rows, cols = ids.shape
    flat = ids.reshape(rows // 2, 2 * cols)
    targets = jnp.arange(cols // 2, dtype=jnp.int32)
    down = (flat[:, None, :] == targets[None, :, None]).astype(jnp.bfloat16)
    up = (flat[:, :, None] == targets).astype(jnp.bfloat16)
    return down, up


def per_device(nlat, nlon, right_side, blocks, kappa, fine_ids, coarse_ids):
    comp, rows, cols = right_side.shape
    lanes = -(-comp // 128) * 128
    tall = -(-comp // 8) * 8
    blocks1, kappa1 = coarsen_tables(blocks, kappa)
    blocks2, kappa2 = coarsen_tables(blocks1, kappa1)
    eye = jnp.eye(comp, dtype=jnp.float32)
    shifted = jnp.concatenate(
        [
            b + 4.0 * k[:, None, None] * eye
            for b, k in ((blocks, kappa), (blocks1, kappa1), (blocks2, kappa2))
        ],
        axis=0,
    )
    total = shifted.shape[0]
    team = TEAM if nlon % TEAM == 0 else 1
    share = -(-total // team)
    batch = -(-share // 8) * 8
    filler = jnp.broadcast_to(eye, (share * (team - 1) + batch - total, comp, comp))
    member = lax.rem(lax.axis_index("lon"), team)
    mine = lax.dynamic_slice_in_dim(
        jnp.concatenate([shifted, filler], axis=0), member * share, batch, axis=0
    )
    stacked = jnp.transpose(mine, (1, 0, 2))
    stacked = jnp.pad(stacked, ((0, tall - comp), (0, 0), (0, lanes - comp)))
    mine = jnp.transpose(invert_stack(stacked, comp)[:, :share], (1, 0, 2))
    teams = [[i + j for j in range(team)] for i in range(0, nlon, team)]
    inverse = lax.all_gather(mine, "lon", axis_index_groups=teams, axis=0, tiled=True)[:total]
    inverse = jnp.pad(inverse, ((0, 0), (0, lanes - tall), (0, 0)))
    top = lax.reduce_precision(inverse, 8, 7)
    low = (inverse - top).astype(jnp.bfloat16)
    top = top.astype(jnp.bfloat16)
    weights = jnp.concatenate([top, top, low], axis=1)
    half, quarter = rows // 2, rows // 4
    w0 = weights[:rows]
    w1 = weights[rows : rows + half]
    w2 = weights[rows + half :]
    m0 = jnp.pad(shifted[:rows], ((0, 0), (0, lanes - comp), (0, lanes - comp)))
    down0, up0 = aggregation_tables(fine_ids)
    down1, up1 = aggregation_tables(coarse_ids)
    rhs = jnp.pad(jnp.transpose(right_side, (1, 2, 0)), ((0, 0), (0, 0), (0, lanes - comp)))

    def field(scale, edged):
        if edged:
            return pltpu.VMEM(
                (rows // scale + 2, cols // scale + 2 * EDGE, lanes), jnp.float32
            )
        return pltpu.VMEM((rows // scale, cols // scale, lanes), jnp.float32)

    vmem = pl.BlockSpec(memory_space=pltpu.VMEM)
    smem = pl.BlockSpec(memory_space=pltpu.SMEM)
    shape = jax.ShapeDtypeStruct(rhs.shape, jnp.float32)
    sol, res = pl.pallas_call(
        functools.partial(cycle_kernel, nlat, nlon),
        out_shape=(shape, shape),
        in_specs=[vmem] * 5 + [smem] * 3 + [vmem] * 4,
        out_specs=(vmem, vmem),
        scratch_shapes=[
            field(1, True), field(1, True), field(2, True), field(2, True),
            field(4, True), field(4, True),
            field(1, False), field(1, False),
            field(2, False), field(2, False), field(2, False),
            field(4, False), field(4, False),
            pltpu.VMEM((2, 2, cols, lanes), jnp.float32),
            pltpu.VMEM((2, 2, rows, lanes), jnp.float32),
            pltpu.VMEM((2, 2, rows, lanes), jnp.float32),
            pltpu.SemaphoreType.DMA((2, 6)),
            pltpu.SemaphoreType.DMA((2, 6)),
        ],
        compiler_params=pltpu.CompilerParams(
            collective_id=0, has_side_effects=True, vmem_limit_bytes=48 * 1024 * 1024
        ),
        name="cycles",
    )(rhs, w0, w1, w2, m0, kappa, kappa1, kappa2, down0, up0, down1, up1)
    return tuple(jnp.transpose(v[:, :, :comp], (2, 0, 1)) for v in (sol, res))


def solution(mesh):
    in_specs = (
        P(None, "lat", "lon"),
        P("lat", None, None),
        P("lat"),
        P("lat", "lon"),
        P("lat", "lon"),
    )
    out_specs = (P(None, "lat", "lon"), P(None, "lat", "lon"))
    return jax.shard_map(
        functools.partial(per_device, mesh.shape["lat"], mesh.shape["lon"]),
        mesh=mesh, in_specs=in_specs, out_specs=out_specs, check_vma=False,
    )
```
